32 devices in a mesh: frame: 8 (over y, x, core), head: 4 (over z).
Axes of the slice: x: 2, y: 2, z: 4, core: 2. Of those that a mesh axis runs over, the one named last changes fastest.
Arguments:
- queries: bfloat16 [4096, 5120], P(('frame', 'head')), may hold values from -6 to 6, as said below
- keys: bfloat16 [4096, 5120], P(('frame', 'head')), may hold values from -6 to 6, as said below
- values: bfloat16 [4096, 5120], P(('frame', 'head')), may hold values from -6 to 6
- q_gain: float32 [5120], replicated, may hold values from 0.5 to 2
- k_gain: float32 [5120], replicated, may hold values from 0.5 to 2
- block_ids: int32 [8, 4, 8], P('frame'), may hold values from 0 to 11, as said below
- counts: int32 [8, 4], P('frame'), may hold values from 1 to 8, as said below
- anchors: int32 [2], replicated, may hold values from 0 to 7, as said below
Outputs:
- attended: bfloat16 [4096, 5120], P(('frame', 'head'))
The draws below stay inside these ranges and needn't reach their ends.
Inputs may be any that keep to these rules, and one draw needn't show every extreme that they name: `queries`: away from rare tokens, entries are of order one. `keys`: away from rare tokens, entries are of order one. `block_ids`: the 8 entries of one list are different; the first is the query block's own block b. `counts`: every view has a query block that uses all 8 listed blocks. `anchors`: the 2 anchor ids are different; one of them is the last view, 7.
All inputs are finite; a program needn't handle non-finite values.
Results may differ from the reference program's by a relative error of at most 0.012.
The reference program's roundings to bfloat16 on the way (of `q_norm`, `k_norm` and `weights`) count: a program that leaves them out, or rounds other values in their place, can miss the bound.
Values may be sent and summed in bfloat16 or wider, within the bound.
A program may use at most 128 MiB of HBM per device.

```python
import math
import jax
import jax.numpy as jnp
from jax import lax

D = 5120
HEADS = 40
HD = 128
BLOCK = 128
KB = 8
ANCHORS = 2
VIEW_TOK = 512
VIEWS = 8
NB = 4
TOKENS = 4096


def draw_queries(key, part):
    key = jax.random.fold_in(key, 21)
    rows = jnp.clip(jax.random.normal(key, (TOKENS, D), jnp.float32), -6.0, 6.0)
    return rows.astype(jnp.bfloat16)


def draw_keys(key, part):
    key = jax.random.fold_in(key, 22)
    rows = jnp.clip(jax.random.normal(key, (TOKENS, D), jnp.float32), -6.0, 6.0)
    return rows.astype(jnp.bfloat16)


def draw_block_ids(key, part):
    key = jax.random.fold_in(key, 11)
    total = (1 + ANCHORS) * NB
    noise = jax.random.randint(key, (VIEWS, NB, total), 0, 4 * NB)
    column = jnp.arange(total, dtype=jnp.int32)
    within = column % NB
    own = jnp.arange(NB, dtype=jnp.int32)
    distance = jnp.abs(within[None, :] - own[:, None])
    score = (4 * distance[None] + noise) * total + column[None, None, :]
    score = jnp.where((column[None, :] == own[:, None])[None], -1, score)
    _, picked = lax.top_k(-score, KB)
    return picked.astype(jnp.int32)


def draw_counts(key, part):
    key = jax.random.fold_in(key, 12)
    first, second, third = jax.random.split(key, 3)
    floor_view = jax.random.randint(first, (VIEWS, 1), 1, KB + 1)
    extra = jax.random.randint(second, (VIEWS, NB), 0, KB // 2 + 1)
    amount = jnp.minimum(floor_view + extra, KB)
    full_block = jax.random.randint(third, (VIEWS,), 0, NB)
    amount = jnp.where(jnp.arange(NB)[None, :] == full_block[:, None], KB, amount)
    return amount.astype(jnp.int32)


def draw_anchors(key, part):
    key = jax.random.fold_in(key, 13)
    first, second = jax.random.split(key, 2)
    others = jax.random.permutation(first, VIEWS - 1)[:ANCHORS].astype(jnp.int32)
    last_slot = jax.random.randint(second, (), 0, ANCHORS)
    places = jnp.arange(ANCHORS, dtype=jnp.int32)
    result = jnp.where(places == last_slot, VIEWS - 1, others)
    return result.astype(jnp.int32)


def levels(key, dims, shards, low, top_value):
    def one(position, parts):
        draws = jax.random.uniform(jax.random.fold_in(jax.random.fold_in(key, 6), position), (parts,), jnp.float32, low / len(shards), top_value / len(shards))
        return jnp.repeat(jnp.exp(draws), dims[position] // parts).reshape((-1,) + (1,) * (len(dims) - position - 1))

    level = one(*shards[0])
    for cut in shards[1:]:
        level = level * one(*cut)
    return level


def centred(own_key, shape, width, most, cuts=(), kind=jnp.bfloat16):
    values = width * jax.random.normal(own_key, shape, jnp.float32)
    if cuts:
        values = values * levels(own_key, shape, cuts, -0.22, 0.18)
    return jnp.clip(values, -most, most).astype(kind)


def setup_inputs(seed: int = 0) -> dict:
    arg_keys = jax.random.split(jax.random.key(seed), 9)
    queries = draw_queries(jax.random.fold_in(arg_keys[8], 71), 0)
    keys = draw_keys(jax.random.fold_in(arg_keys[8], 71), 0)
    values = centred(arg_keys[2], (TOKENS, D), 1.0, 6.0, ((0, 32),))
    q_gain = jnp.clip(jnp.exp(jax.random.uniform(arg_keys[3], (D,), jnp.float32, math.log(0.5), math.log(2.0))), 0.5, 2.0)
    k_gain = jnp.clip(jnp.exp(jax.random.uniform(arg_keys[4], (D,), jnp.float32, math.log(0.5), math.log(2.0))), 0.5, 2.0)
    block_ids = draw_block_ids(jax.random.fold_in(arg_keys[8], 71), 0)
    counts = draw_counts(jax.random.fold_in(arg_keys[8], 71), 0)
    anchors = draw_anchors(jax.random.fold_in(arg_keys[8], 71), 0)
    return {"queries": queries, "keys": keys, "values": values, "q_gain": q_gain, "k_gain": k_gain, "block_ids": block_ids, "counts": counts, "anchors": anchors}


def normalize(rows, gain):
    wide = rows.astype(jnp.float32)
    square = lax.optimization_barrier(jnp.mean(wide * wide, axis=-1, keepdims=True))
    return (wide * lax.rsqrt(square + 1e-06) * gain).astype(jnp.bfloat16)

def reference(queries, keys, values, q_gain, k_gain, block_ids, counts, anchors):
    views = TOKENS // VIEW_TOK
    blocks = VIEW_TOK // BLOCK
    q_norm = normalize(queries, q_gain).reshape(views, VIEW_TOK, HEADS, HD)
    k_norm = normalize(keys, k_gain).reshape(views, VIEW_TOK, HEADS, HD)
    v_rows = values.reshape(views, VIEW_TOK, HEADS, HD)
    anchor_k = jnp.take(k_norm, anchors, axis=0).reshape(ANCHORS * blocks, BLOCK, HEADS, HD)
    anchor_v = jnp.take(v_rows, anchors, axis=0).reshape(ANCHORS * blocks, BLOCK, HEADS, HD)
    scale = 1.0 / math.sqrt(HD)
    slots = jnp.arange(KB, dtype=jnp.int32)

    def one_view(args):
        q_view, k_view, v_view, id_view, count_view = args
        key_blocks = jnp.concatenate([k_view.reshape(blocks, BLOCK, HEADS, HD), anchor_k], axis=0)
        value_blocks = jnp.concatenate([v_view.reshape(blocks, BLOCK, HEADS, HD), anchor_v], axis=0)

        def one_block(inner):
            q_block, id_list, count = inner
            picked_k = key_blocks[id_list].astype(jnp.float32)
            picked_v = value_blocks[id_list].astype(jnp.float32)
            scores = jnp.einsum('qhd,kphd->hqkp', q_block.astype(jnp.float32), picked_k) * scale
            valid = (slots < count)[None, None, :, None]
            scores = jnp.where(valid, scores, -1e+30)
            top = lax.optimization_barrier(jnp.max(scores, axis=(2, 3), keepdims=True))
            expo = jnp.exp(scores - top)
            weights = (expo / lax.optimization_barrier(jnp.sum(expo, axis=(2, 3), keepdims=True))).astype(jnp.bfloat16)
            mixed = jnp.einsum('hqkp,kphd->qhd', weights.astype(jnp.float32), picked_v)
            return mixed.astype(jnp.bfloat16)
        return lax.map(one_block, (q_view.reshape(blocks, BLOCK, HEADS, HD), id_view, count_view))
    result = lax.map(one_view, (q_norm, k_norm, v_rows, block_ids, counts))
    return result.reshape(TOKENS, D)
```

```python
import functools
import math

import jax
import jax.numpy as jnp
from jax import lax
from jax.experimental import pallas as pl
from jax.experimental.pallas import tpu as pltpu
from jax.sharding import PartitionSpec as P

HD = 128
BLOCK = 128
WINDOW = 3
EPS = 1e-06
MESH = pl.DeviceIdType.MESH


def columns(head):
    return pl.ds(pl.multiple_of(head * HD, HD), HD)


def kernel(
    nz, nf, bits, heads, anchor_total, listed,
    ids_ref, counts_ref, anchors_ref, q_ref, k_ref, v_ref, qg_ref, kg_ref, out_ref,
    qn, kn, kv, qb, core_in, hop_out, hop_in, mixed, bias,
    in_send, in_recv, core_send, core_recv, hop_send, hop_recv, pair_send, pair_recv, out_send, out_recv,
):
    f = lax.axis_index("frame")
    z = lax.axis_index("head")
    all_heads = nz * heads
    total = nz * (1 + anchor_total)
    hops = bits - 1
    me_bits = [lax.rem(lax.div(f, 2**k), 2) for k in range(bits)]
    partners = [f + (2**k) * (1 - 2 * me_bits[k]) for k in range(bits)]
    core = me_bits[0]

    barrier = pltpu.get_barrier_semaphore()
    for d in range(1, nz):
        pl.semaphore_signal(barrier, inc=1, device_id={"head": lax.rem(z + d, nz)}, device_id_type=MESH)
    for k in range(bits):
        pl.semaphore_signal(barrier, inc=1, device_id={"frame": partners[k]}, device_id_type=MESH)

    def in_copy(kind, j, d):
        to = lax.rem(z + d, nz)
        head = to * heads + j
        if kind == 0:
            src, dst = kn.at[head], kv.at[0, j, z]
        elif kind == 1:
            src, dst = v_ref.at[:, columns(head)], kv.at[1, j, z]
        else:
            src, dst = qn.at[head], qb.at[j, z]
        return pltpu.make_async_remote_copy(
            src_ref=src, dst_ref=dst, send_sem=in_send.at[kind, j, d], recv_sem=in_recv.at[kind, j, d],
            device_id={"head": to}, device_id_type=MESH,
        )

    def out_copy(j, d):
        to = lax.rem(z + d, nz)
        return pltpu.make_async_remote_copy(
            src_ref=mixed.at[j, to], dst_ref=out_ref.at[:, columns(z * heads + j)],
            send_sem=out_send.at[j, d], recv_sem=out_recv.at[j, d],
            device_id={"head": to}, device_id_type=MESH,
        )

    def core_copy(j):
        return pltpu.make_async_remote_copy(
            src_ref=kv.at[1 - core, j, pl.ds(0, nz)], dst_ref=core_in.at[j],
            send_sem=core_send.at[j], recv_sem=core_recv.at[j],
            device_id={"frame": partners[0]}, device_id_type=MESH,
        )

    def hop_copy(k, j):
        return pltpu.make_async_remote_copy(
            src_ref=hop_out.at[k, j], dst_ref=hop_in.at[k, j],
            send_sem=hop_send.at[k, j], recv_sem=hop_recv.at[k, j],
            device_id={"frame": partners[k + 1]}, device_id_type=MESH,
        )

    def pair_copy(j):
        far = kv.at[core, j, pl.ds(nz, nz * anchor_total)]
        return pltpu.make_async_remote_copy(
            src_ref=far, dst_ref=far, send_sem=pair_send.at[j], recv_sem=pair_recv.at[j],
            device_id={"frame": partners[0]}, device_id_type=MESH,
        )

    def kinds_of(unit, act):
        @pl.when(unit < heads)
        def _():
            for kind in (0, 1):
                for d in range(1, nz):
                    act(in_copy(kind, unit, d))

        @pl.when(unit >= heads)
        def _():
            for d in range(1, nz):
                act(in_copy(2, unit - heads, d))

    def send_unit(unit):
        kinds_of(unit, lambda copy: copy.start())

    def unit_sent(unit):
        kinds_of(unit, lambda copy: copy.wait_send())

    def normalize(src, gain, dst):
        def square(h, acc):
            wide = src[:, columns(h)].astype(jnp.float32)
            return acc + wide * wide

        acc = lax.fori_loop(0, all_heads, square, jnp.zeros((BLOCK, HD), jnp.float32))
        mean = jnp.sum(acc, axis=1, keepdims=True) * (1.0 / (all_heads * HD))
        factor = lax.rsqrt(mean + EPS)

        def write(h, carry):
            wide = src[:, columns(h)].astype(jnp.float32)
            dst[h] = (wide * factor * gain[:, columns(h)]).astype(jnp.bfloat16)
            return carry

        lax.fori_loop(0, all_heads, write, 0)

    normalize(k_ref, kg_ref, kn)
    pl.semaphore_wait(barrier, nz - 1 + bits)
    for unit in range(WINDOW):
        send_unit(jnp.int32(unit))
    normalize(q_ref, qg_ref, qn)

    def own(j, carry):
        head = z * heads + j
        kv[0, j, z] = kn[head]
        kv[1, j, z] = v_ref[:, columns(head)]
        qb[j, z] = qn[head]
        return carry

    lax.fori_loop(0, heads, own, 0)

    for b in range(nz):
        count = counts_ref[0, b]
        wanted = [lax.select(count > s, ids_ref[0, b, s], jnp.int32(-1)) for s in range(listed)]
        for c in range(total):
            hit = wanted[0] == c
            for s in range(1, listed):
                hit = jnp.logical_or(hit, wanted[s] == c)
            value = lax.select(hit, jnp.float32(0.0), jnp.float32(-1e30))
            bias[b, :, c * BLOCK:(c + 1) * BLOCK] = jnp.full((8, BLOCK), value, jnp.float32)

    def mine(a, k):
        bit = lax.rem(lax.div(anchors_ref[a], jnp.int32(2**k)), jnp.int32(2))
        return bit == me_bits[k]

    flags = [[mine(a, k) for k in range(bits)] for a in range(anchor_total)]
    scale = 1.0 / math.sqrt(HD)
    first = max(heads, 2 * hops)

    def step(t, carry):
        @pl.when(t + WINDOW < 2 * heads)
        def _():
            @pl.when(t < heads)
            def _():
                for kind in (0, 1):
                    for d in range(1, nz):
                        in_copy(kind, t, d).wait_recv()

            send_unit(t + WINDOW)

        @pl.when(jnp.logical_and(t < heads, t + WINDOW >= 2 * heads))
        def _():
            for kind in (0, 1):
                for d in range(1, nz):
                    in_copy(kind, t, d).wait_recv()

        @pl.when(t < heads)
        def _():
            core_copy(t).start()

        for k in reversed(range(hops)):
            j = t - 2 * (k + 1)

            @pl.when(jnp.logical_and(j >= 0, j < heads))
            def _():
                hop_copy(k, j).wait_recv()
                for a in range(anchor_total):
                    for n in range(nz):
                        picked = lax.select_n(flags[a][k + 1], hop_in[k, j, a, n], hop_out[k, j, a, n])
                        if k == hops - 1:
                            kv[core, j, nz * (1 + a) + n] = picked
                        else:
                            hop_out[k + 1, j, a, n] = picked
                if k == hops - 1:
                    pair_copy(j).start()
                else:
                    hop_copy(k + 1, j).start()

        @pl.when(t < heads)
        def _():
            core_copy(t).wait_recv()
            for a in range(anchor_total):
                for n in range(nz):
                    hop_out[0, t, a, n] = lax.select_n(flags[a][0], core_in[t, n], kv[core, t, n])
            hop_copy(0, t).start()

        @pl.when(t >= first)
        def _():
            e = t - first
            for d in range(1, nz):
                in_copy(2, e, d).wait_recv()
            pair_copy(e).wait_recv()

            def attend(b, inner):
                k_all = kv[0, e].reshape(total * BLOCK, HD)
                v_all = kv[1, e].reshape(total * BLOCK, HD)
                scores = lax.dot_general(
                    qb[e, b], k_all, (((1,), (1,)), ((), ())), preferred_element_type=jnp.float32
                )
                scores = scores * scale + bias[b, 0:1, :]
                top = jnp.max(scores, axis=1, keepdims=True)
                expo = jnp.exp(scores - top)
                weights = (expo * (1.0 / jnp.sum(expo, axis=1, keepdims=True))).astype(jnp.bfloat16)
                mixed[e, b] = jnp.dot(weights, v_all, preferred_element_type=jnp.float32).astype(jnp.bfloat16)
                return inner

            lax.fori_loop(0, nz, attend, 0)
            for d in range(1, nz):
                out_copy(e, d).start()
            out_ref[:, columns(z * heads + e)] = mixed[e, z]
            unit_sent(2 * e)
            unit_sent(2 * e + 1)
            core_copy(e).wait_send()
            for k in range(hops):
                hop_copy(k, e).wait_send()
            pair_copy(e).wait_send()

            @pl.when(e >= 2)
            def _():
                for d in range(1, nz):
                    out_copy(e - 2, d).wait_send()

        return carry

    lax.fori_loop(0, first + heads, step, 0)

    for e in range(max(heads - 2, 0), heads):
        for d in range(1, nz):
            out_copy(e, d).wait_send()

    def arrived(e, carry):
        for d in range(1, nz):
            out_copy(e, d).wait_recv()
        return carry

    lax.fori_loop(0, heads, arrived, 0)


def shards(nz, nf, queries, keys, values, q_gain, k_gain, block_ids, counts, anchors):
    rows, width = queries.shape
    bits = nf.bit_length() - 1
    hops = bits - 1
    all_heads = width // HD
    heads = all_heads // nz
    anchor_total = anchors.shape[0]
    total = nz * (1 + anchor_total)
    listed = block_ids.shape[2]
    tile = (BLOCK, HD)
    bf = jnp.bfloat16
    dma = pltpu.SemaphoreType.DMA
    smem = pl.BlockSpec(memory_space=pltpu.SMEM)
    vmem = pl.BlockSpec(memory_space=pltpu.VMEM)
    return pl.pallas_call(
        functools.partial(kernel, nz, nf, bits, heads, anchor_total, listed),
        out_shape=jax.ShapeDtypeStruct((rows, width), bf),
        in_specs=[smem] * 3 + [vmem] * 5,
        out_specs=vmem,
        scratch_shapes=[
            pltpu.VMEM((all_heads,) + tile, bf),
            pltpu.VMEM((all_heads,) + tile, bf),
            pltpu.VMEM((2, heads, total) + tile, bf),
            pltpu.VMEM((heads, nz) + tile, bf),
            pltpu.VMEM((heads, nz) + tile, bf),
            pltpu.VMEM((hops, heads, anchor_total, nz) + tile, bf),
            pltpu.VMEM((hops, heads, anchor_total, nz) + tile, bf),
            pltpu.VMEM((heads, nz) + tile, bf),
            pltpu.VMEM((nz, 8, total * BLOCK), jnp.float32),
            dma((3, heads, nz)),
            dma((3, heads, nz)),
            dma((heads,)),
            dma((heads,)),
            dma((hops, heads)),
            dma((hops, heads)),
            dma((heads,)),
            dma((heads,)),
            dma((heads, nz)),
            dma((heads, nz)),
        ],
        compiler_params=pltpu.CompilerParams(
            collective_id=0, has_side_effects=True, vmem_limit_bytes=56 * 1024 * 1024
        ),
    )(block_ids, counts, anchors, queries, keys, values, q_gain[None, :], k_gain[None, :])


def solution(mesh):
    placed = (
        P(("frame", "head"), None),
        P(("frame", "head"), None),
        P(("frame", "head"), None),
        P(),
        P(),
        P("frame", None, None),
        P("frame", None),
        P(),
    )
    return jax.shard_map(
        functools.partial(shards, mesh.shape["head"], mesh.shape["frame"]),
        mesh=mesh, in_specs=placed, out_specs=P(("frame", "head"), None), check_vma=False,
    )
```

```python
import functools
import math

import jax
import jax.numpy as jnp
from jax import lax
from jax.experimental import pallas as pl
from jax.experimental.pallas import tpu as pltpu
from jax.sharding import PartitionSpec as P

HD = 128
BLOCK = 128
WINDOW = 3
EPS = 1e-06
MESH = pl.DeviceIdType.MESH


def columns(head):
    return pl.ds(pl.multiple_of(head * HD, HD), HD)


def kernel(
    nz, nf, bits, heads, anchor_total, listed,
    ids_ref, counts_ref, anchors_ref, q_hbm, k_hbm, v_hbm, qg_ref, kg_ref, out_ref,
    q_ref, k_ref, v_ref, load_sem, qn, kn, kv, qb, core_in, hop_out, hop_in, mixed, bias,
    in_send, in_recv, core_send, core_recv, hop_send, hop_recv, pair_send, pair_recv, out_send, out_recv,
):
    f = lax.axis_index("frame")
    z = lax.axis_index("head")
    all_heads = nz * heads
    total = nz * (1 + anchor_total)
    hops = bits - 1
    me_bits = [lax.rem(lax.div(f, 2**k), 2) for k in range(bits)]
    partners = [f + (2**k) * (1 - 2 * me_bits[k]) for k in range(bits)]
    core = me_bits[0]

    loads = [
        pltpu.make_async_copy(src, dst, load_sem.at[n])
        for n, (src, dst) in enumerate(((v_hbm, v_ref), (k_hbm, k_ref), (q_hbm, q_ref)))
    ]
    for load in loads:
        load.start()
    barrier = pltpu.get_barrier_semaphore()
    for d in range(1, nz):
        pl.semaphore_signal(barrier, inc=1, device_id={"head": lax.rem(z + d, nz)}, device_id_type=MESH)
    for k in range(bits):
        pl.semaphore_signal(barrier, inc=1, device_id={"frame": partners[k]}, device_id_type=MESH)

    def in_copy(kind, j, d):
        to = lax.rem(z + d, nz)
        head = to * heads + j
        if kind == 0:
            src, dst = kn.at[head], kv.at[0, j, z]
        elif kind == 1:
            src, dst = v_ref.at[:, columns(head)], kv.at[1, j, z]
        else:
            src, dst = qn.at[head], qb.at[j, z]
        return pltpu.make_async_remote_copy(
            src_ref=src, dst_ref=dst, send_sem=in_send.at[kind, j, d], recv_sem=in_recv.at[kind, j, d],
            device_id={"head": to}, device_id_type=MESH,
        )

    def out_copy(j, d):
        to = lax.rem(z + d, nz)
        return pltpu.make_async_remote_copy(
            src_ref=mixed.at[j, to], dst_ref=out_ref.at[:, columns(z * heads + j)],
            send_sem=out_send.at[j, d], recv_sem=out_recv.at[j, d],
            device_id={"head": to}, device_id_type=MESH,
        )

    def core_copy(j):
        return pltpu.make_async_remote_copy(
            src_ref=kv.at[1 - core, j, pl.ds(0, nz)], dst_ref=core_in.at[j],
            send_sem=core_send.at[j], recv_sem=core_recv.at[j],
            device_id={"frame": partners[0]}, device_id_type=MESH,
        )

    def hop_copy(k, j):
        return pltpu.make_async_remote_copy(
            src_ref=hop_out.at[k, j], dst_ref=hop_in.at[k, j],
            send_sem=hop_send.at[k, j], recv_sem=hop_recv.at[k, j],
            device_id={"frame": partners[k + 1]}, device_id_type=MESH,
        )

    def pair_copy(j):
        far = kv.at[core, j, pl.ds(nz, nz * anchor_total)]
        return pltpu.make_async_remote_copy(
            src_ref=far, dst_ref=far, send_sem=pair_send.at[j], recv_sem=pair_recv.at[j],
            device_id={"frame": partners[0]}, device_id_type=MESH,
        )

    def kinds_of(unit, act):
        @pl.when(unit < heads)
        def _():
            for kind in (1, 0):
                for d in range(1, nz):
                    act(in_copy(kind, unit, d))

        @pl.when(unit >= heads)
        def _():
            for d in range(1, nz):
                act(in_copy(2, unit - heads, d))

    def send_unit(unit):
        kinds_of(unit, lambda copy: copy.start())

    def unit_sent(unit):
        kinds_of(unit, lambda copy: copy.wait_send())

    def normalize(src, gain, dst):
        def square(h, acc):
            wide = src[:, columns(h)].astype(jnp.float32)
            return acc + wide * wide

        acc = lax.fori_loop(0, all_heads, square, jnp.zeros((BLOCK, HD), jnp.float32))
        mean = jnp.sum(acc, axis=1, keepdims=True) * (1.0 / (all_heads * HD))
        factor = lax.rsqrt(mean + EPS)

        def write(h, carry):
            wide = src[:, columns(h)].astype(jnp.float32)
            dst[h] = (wide * factor * gain[:, columns(h)]).astype(jnp.bfloat16)
            return carry

        lax.fori_loop(0, all_heads, write, 0)

    loads[0].wait()
    pl.semaphore_wait(barrier, nz - 1 + bits)
    for unit in range(WINDOW):
        for d in range(1, nz):
            in_copy(1, unit, d).start()
    loads[1].wait()
    normalize(k_ref, kg_ref, kn)
    for unit in range(WINDOW):
        for d in range(1, nz):
            in_copy(0, unit, d).start()
    loads[2].wait()
    normalize(q_ref, qg_ref, qn)

    def own(j, carry):
        head = z * heads + j
        kv[0, j, z] = kn[head]
        kv[1, j, z] = v_ref[:, columns(head)]
        qb[j, z] = qn[head]
        return carry

    lax.fori_loop(0, heads, own, 0)

    for b in range(nz):
        count = counts_ref[0, b]
        wanted = [lax.select(count > s, ids_ref[0, b, s], jnp.int32(-1)) for s in range(listed)]
        for c in range(total):
            hit = wanted[0] == c
            for s in range(1, listed):
                hit = jnp.logical_or(hit, wanted[s] == c)
            value = lax.select(hit, jnp.float32(0.0), jnp.float32(-1e30))
            bias[b, :, c * BLOCK:(c + 1) * BLOCK] = jnp.full((8, BLOCK), value, jnp.float32)

    def mine(a, k):
        bit = lax.rem(lax.div(anchors_ref[a], jnp.int32(2**k)), jnp.int32(2))
        return bit == me_bits[k]

    flags = [[mine(a, k) for k in range(bits)] for a in range(anchor_total)]
    scale = math.log2(math.e) / math.sqrt(HD)
    first = max(heads, 2 * hops)

    def step(t, carry):
        @pl.when(t + WINDOW < 2 * heads)
        def _():
            @pl.when(t < heads)
            def _():
                for kind in (0, 1):
                    for d in range(1, nz):
                        in_copy(kind, t, d).wait_recv()

            send_unit(t + WINDOW)

        @pl.when(jnp.logical_and(t < heads, t + WINDOW >= 2 * heads))
        def _():
            for kind in (0, 1):
                for d in range(1, nz):
                    in_copy(kind, t, d).wait_recv()

        @pl.when(t < heads)
        def _():
            core_copy(t).start()

        for k in reversed(range(hops)):
            j = t - 2 * (k + 1)

            @pl.when(jnp.logical_and(j >= 0, j < heads))
            def _():
                hop_copy(k, j).wait_recv()
                for a in range(anchor_total):
                    for n in range(nz):
                        picked = lax.select_n(flags[a][k + 1], hop_in[k, j, a, n], hop_out[k, j, a, n])
                        if k == hops - 1:
                            kv[core, j, nz * (1 + a) + n] = picked
                        else:
                            hop_out[k + 1, j, a, n] = picked
                if k == hops - 1:
                    pair_copy(j).start()
                else:
                    hop_copy(k + 1, j).start()

        @pl.when(t < heads)
        def _():
            core_copy(t).wait_recv()
            for a in range(anchor_total):
                for n in range(nz):
                    hop_out[0, t, a, n] = lax.select_n(flags[a][0], core_in[t, n], kv[core, t, n])
            hop_copy(0, t).start()

        @pl.when(t >= first)
        def _():
            e = t - first
            for d in range(1, nz):
                in_copy(2, e, d).wait_recv()
            pair_copy(e).wait_recv()

            def attend(i, inner):
                b = lax.rem(z + 1 + i, nz)
                k_all = kv[0, e].reshape(total * BLOCK, HD)
                v_all = kv[1, e].reshape(total * BLOCK, HD)
                scores = lax.dot_general(
                    qb[e, b], k_all, (((1,), (1,)), ((), ())), preferred_element_type=jnp.float32
                )
                scores = scores * scale + bias[b, 0:1, :]
                top = jnp.max(scores, axis=1, keepdims=True)
                expo = jnp.exp2(scores - top)
                weights = (expo * (1.0 / jnp.sum(expo, axis=1, keepdims=True))).astype(jnp.bfloat16)
                mixed[e, b] = jnp.dot(weights, v_all, preferred_element_type=jnp.float32).astype(jnp.bfloat16)

                @pl.when(i < nz - 1)
                def _():
                    out_copy(e, i + 1).start()

                return inner

            lax.fori_loop(0, nz, attend, 0)
            out_ref[:, columns(z * heads + e)] = mixed[e, z]
            unit_sent(2 * e)
            unit_sent(2 * e + 1)
            core_copy(e).wait_send()
            for k in range(hops):
                hop_copy(k, e).wait_send()
            pair_copy(e).wait_send()

            @pl.when(e >= 2)
            def _():
                for d in range(1, nz):
                    out_copy(e - 2, d).wait_send()

        return carry

    lax.fori_loop(0, first + heads, step, 0)

    for e in range(max(heads - 2, 0), heads):
        for d in range(1, nz):
            out_copy(e, d).wait_send()

    def arrived(e, carry):
        for d in range(1, nz):
            out_copy(e, d).wait_recv()
        return carry

    lax.fori_loop(0, heads, arrived, 0)


def shards(nz, nf, queries, keys, values, q_gain, k_gain, block_ids, counts, anchors):
    rows, width = queries.shape
    bits = nf.bit_length() - 1
    hops = bits - 1
    all_heads = width // HD
    heads = all_heads // nz
    anchor_total = anchors.shape[0]
    total = nz * (1 + anchor_total)
    listed = block_ids.shape[2]
    tile = (BLOCK, HD)
    bf = jnp.bfloat16
    dma = pltpu.SemaphoreType.DMA
    smem = pl.BlockSpec(memory_space=pltpu.SMEM)
    vmem = pl.BlockSpec(memory_space=pltpu.VMEM)
    return pl.pallas_call(
        functools.partial(kernel, nz, nf, bits, heads, anchor_total, listed),
        out_shape=jax.ShapeDtypeStruct((rows, width), bf),
        in_specs=[smem] * 3 + [pl.BlockSpec(memory_space=pl.ANY)] * 3 + [vmem] * 2,
        out_specs=vmem,
        scratch_shapes=[
            pltpu.VMEM((rows, width), bf),
            pltpu.VMEM((rows, width), bf),
            pltpu.VMEM((rows, width), bf),
            dma((3,)),
            pltpu.VMEM((all_heads,) + tile, bf),
            pltpu.VMEM((all_heads,) + tile, bf),
            pltpu.VMEM((2, heads, total) + tile, bf),
            pltpu.VMEM((heads, nz) + tile, bf),
            pltpu.VMEM((heads, nz) + tile, bf),
            pltpu.VMEM((hops, heads, anchor_total, nz) + tile, bf),
            pltpu.VMEM((hops, heads, anchor_total, nz) + tile, bf),
            pltpu.VMEM((heads, nz) + tile, bf),
            pltpu.VMEM((nz, 8, total * BLOCK), jnp.float32),
            dma((3, heads, nz)),
            dma((3, heads, nz)),
            dma((heads,)),
            dma((heads,)),
            dma((hops, heads)),
            dma((hops, heads)),
            dma((heads,)),
            dma((heads,)),
            dma((heads, nz)),
            dma((heads, nz)),
        ],
        compiler_params=pltpu.CompilerParams(
            collective_id=0, has_side_effects=True, vmem_limit_bytes=56 * 1024 * 1024
        ),
    )(block_ids, counts, anchors, queries, keys, values, q_gain[None, :], k_gain[None, :])


def solution(mesh):
    placed = (
        P(("frame", "head"), None),
        P(("frame", "head"), None),
        P(("frame", "head"), None),
        P(),
        P(),
        P("frame", None, None),
        P("frame", None),
        P(),
    )
    return jax.shard_map(
        functools.partial(shards, mesh.shape["head"], mesh.shape["frame"]),
        mesh=mesh, in_specs=placed, out_specs=P(("frame", "head"), None), check_vma=False,
    )
```

```python
import functools
import math

import jax
import jax.numpy as jnp
from jax import lax
from jax.experimental import pallas as pl
from jax.experimental.pallas import tpu as pltpu
from jax.sharding import PartitionSpec as P

HD = 128
BLOCK = 128
WINDOW = 5
EPS = 1e-06
MESH = pl.DeviceIdType.MESH


def columns(head):
    return pl.ds(pl.multiple_of(head * HD, HD), HD)


def kernel(
    nz, nf, bits, heads, anchor_total, listed,
    ids_ref, counts_ref, anchors_ref, q_hbm, k_hbm, v_hbm, qg_ref, kg_ref, out_ref,
    q_ref, k_ref, v_ref, load_sem, qn, kn, kv, qb, core_in, hop_out, hop_in, mixed, bias,
    in_send, in_recv, core_send, core_recv, hop_send, hop_recv, pair_send, pair_recv, out_send, out_recv,
):
    f = lax.axis_index("frame")
    z = lax.axis_index("head")
    all_heads = nz * heads
    total = nz * (1 + anchor_total)
    hops = bits - 1
    me_bits = [lax.rem(lax.div(f, 2**k), 2) for k in range(bits)]
    partners = [f + (2**k) * (1 - 2 * me_bits[k]) for k in range(bits)]
    core = me_bits[0]
    window = min(WINDOW, heads)

    loads = [
        pltpu.make_async_copy(src, dst, load_sem.at[n])
        for n, (src, dst) in enumerate(((v_hbm, v_ref), (k_hbm, k_ref), (q_hbm, q_ref)))
    ]
    for load in loads:
        load.start()
    barrier = pltpu.get_barrier_semaphore()
    for d in range(1, nz):
        pl.semaphore_signal(barrier, inc=1, device_id={"head": lax.rem(z + d, nz)}, device_id_type=MESH)
    for k in range(bits):
        pl.semaphore_signal(barrier, inc=1, device_id={"frame": partners[k]}, device_id_type=MESH)

    def in_copy(kind, j, d):
        to = lax.rem(z + d, nz)
        head = to * heads + j
        if kind == 0:
            src, dst = kn.at[head], kv.at[0, j, z]
        elif kind == 1:
            src, dst = v_ref.at[:, columns(head)], kv.at[1, j, z]
        else:
            src, dst = qn.at[head], qb.at[j, z]
        return pltpu.make_async_remote_copy(
            src_ref=src, dst_ref=dst, send_sem=in_send.at[kind, j, d], recv_sem=in_recv.at[kind, j, d],
            device_id={"head": to}, device_id_type=MESH,
        )

    def out_copy(j, d):
        to = lax.rem(z + d, nz)
        return pltpu.make_async_remote_copy(
            src_ref=mixed.at[j, to], dst_ref=out_ref.at[:, columns(z * heads + j)],
            send_sem=out_send.at[j, d], recv_sem=out_recv.at[j, d],
            device_id={"head": to}, device_id_type=MESH,
        )

    def core_copy(j):
        return pltpu.make_async_remote_copy(
            src_ref=kv.at[1 - core, j, pl.ds(0, nz)], dst_ref=core_in.at[j],
            send_sem=core_send.at[j], recv_sem=core_recv.at[j],
            device_id={"frame": partners[0]}, device_id_type=MESH,
        )

    def hop_copy(k, j):
        return pltpu.make_async_remote_copy(
            src_ref=hop_out.at[k, j], dst_ref=hop_in.at[k, j],
            send_sem=hop_send.at[k, j], recv_sem=hop_recv.at[k, j],
            device_id={"frame": partners[k + 1]}, device_id_type=MESH,
        )

    def pair_copy(j):
        far = kv.at[core, j, pl.ds(nz, nz * anchor_total)]
        return pltpu.make_async_remote_copy(
            src_ref=far, dst_ref=far, send_sem=pair_send.at[j], recv_sem=pair_recv.at[j],
            device_id={"frame": partners[0]}, device_id_type=MESH,
        )

    def kinds_of(unit, act):
        @pl.when(unit < heads)
        def _():
            for kind in (1, 0):
                for d in range(1, nz):
                    act(in_copy(kind, unit, d))

        @pl.when(unit >= heads)
        def _():
            for d in range(1, nz):
                act(in_copy(2, unit - heads, d))

    def send_unit(unit):
        kinds_of(unit, lambda copy: copy.start())

    def unit_sent(unit):
        kinds_of(unit, lambda copy: copy.wait_send())

    def normalize(src, gain, dst):
        def square(h, acc):
            wide = src[:, columns(h)].astype(jnp.float32)
            return acc + wide * wide

        acc = lax.fori_loop(0, all_heads, square, jnp.zeros((BLOCK, HD), jnp.float32))
        mean = jnp.sum(acc, axis=1, keepdims=True) * (1.0 / (all_heads * HD))
        factor = lax.rsqrt(mean + EPS)

        def write(h, carry):
            wide = src[:, columns(h)].astype(jnp.float32)
            dst[h] = (wide * factor * gain[:, columns(h)]).astype(jnp.bfloat16)
            return carry

        lax.fori_loop(0, all_heads, write, 0)

    loads[0].wait()
    pl.semaphore_wait(barrier, nz - 1 + bits)
    for unit in range(window):
        for d in range(1, nz):
            in_copy(1, unit, d).start()
    loads[1].wait()
    normalize(k_ref, kg_ref, kn)
    for unit in range(window):
        for d in range(1, nz):
            in_copy(0, unit, d).start()
    loads[2].wait()
    normalize(q_ref, qg_ref, qn)

    def own(j, carry):
        head = z * heads + j
        kv[0, j, z] = kn[head]
        kv[1, j, z] = v_ref[:, columns(head)]
        qb[j, z] = qn[head]
        return carry

    lax.fori_loop(0, heads, own, 0)

    for b in range(nz):
        count = counts_ref[0, b]
        wanted = [lax.select(count > s, ids_ref[0, b, s], jnp.int32(-1)) for s in range(listed)]
        for c in range(total):
            hit = wanted[0] == c
            for s in range(1, listed):
                hit = jnp.logical_or(hit, wanted[s] == c)
            value = lax.select(hit, jnp.float32(0.0), jnp.float32(-1e30))
            bias[b, :, c * BLOCK:(c + 1) * BLOCK] = jnp.full((8, BLOCK), value, jnp.float32)

    def mine(a, k):
        bit = lax.rem(lax.div(anchors_ref[a], jnp.int32(2**k)), jnp.int32(2))
        return bit == me_bits[k]

    flags = [[mine(a, k) for k in range(bits)] for a in range(anchor_total)]
    scale = math.log2(math.e) / math.sqrt(HD)
    first = max(heads, 2 * hops)

    def step(t, carry):
        @pl.when(t + window < 2 * heads)
        def _():
            @pl.when(t < heads)
            def _():
                for kind in (0, 1):
                    for d in range(1, nz):
                        in_copy(kind, t, d).wait_recv()

            send_unit(t + window)

        @pl.when(jnp.logical_and(t < heads, t + window >= 2 * heads))
        def _():
            for kind in (0, 1):
                for d in range(1, nz):
                    in_copy(kind, t, d).wait_recv()

        @pl.when(t < heads)
        def _():
            core_copy(t).start()

        for k in reversed(range(hops)):
            j = t - 2 * (k + 1)

            @pl.when(jnp.logical_and(j >= 0, j < heads))
            def _():
                hop_copy(k, j).wait_recv()
                for a in range(anchor_total):
                    for n in range(nz):
                        picked = lax.select_n(flags[a][k + 1], hop_in[k, j, a, n], hop_out[k, j, a, n])
                        if k == hops - 1:
                            kv[core, j, nz * (1 + a) + n] = picked
                        else:
                            hop_out[k + 1, j, a, n] = picked
                if k == hops - 1:
                    pair_copy(j).start()
                else:
                    hop_copy(k + 1, j).start()

        @pl.when(t < heads)
        def _():
            core_copy(t).wait_recv()
            for a in range(anchor_total):
                for n in range(nz):
                    hop_out[0, t, a, n] = lax.select_n(flags[a][0], core_in[t, n], kv[core, t, n])
            hop_copy(0, t).start()

        @pl.when(t >= first)
        def _():
            e = t - first
            for d in range(1, nz):
                in_copy(2, e, d).wait_recv()
            pair_copy(e).wait_recv()

            def attend(i, inner):
                b = lax.rem(z + 1 + i, nz)
                k_all = kv[0, e].reshape(total * BLOCK, HD)
                v_all = kv[1, e].reshape(total * BLOCK, HD)
                scores = lax.dot_general(
                    qb[e, b], k_all, (((1,), (1,)), ((), ())), preferred_element_type=jnp.float32
                )
                scores = scores * scale + bias[b, 0:1, :]
                top = jnp.max(scores, axis=1, keepdims=True)
                expo = jnp.exp2(scores - top)
                weights = (expo * (1.0 / jnp.sum(expo, axis=1, keepdims=True))).astype(jnp.bfloat16)
                mixed[e, b] = jnp.dot(weights, v_all, preferred_element_type=jnp.float32).astype(jnp.bfloat16)

                @pl.when(i < nz - 1)
                def _():
                    out_copy(e, i + 1).start()

                return inner

            lax.fori_loop(0, nz, attend, 0)
            out_ref[:, columns(z * heads + e)] = mixed[e, z]
            unit_sent(2 * e)
            unit_sent(2 * e + 1)
            core_copy(e).wait_send()
            for k in range(hops):
                hop_copy(k, e).wait_send()
            pair_copy(e).wait_send()

            @pl.when(e >= 2)
            def _():
                for d in range(1, nz):
                    out_copy(e - 2, d).wait_send()

        return carry

    lax.fori_loop(0, first + heads, step, 0)

    for e in range(max(heads - 2, 0), heads):
        for d in range(1, nz):
            out_copy(e, d).wait_send()

    def arrived(e, carry):
        for d in range(1, nz):
            out_copy(e, d).wait_recv()
        return carry

    lax.fori_loop(0, heads, arrived, 0)


def shards(nz, nf, queries, keys, values, q_gain, k_gain, block_ids, counts, anchors):
    rows, width = queries.shape
    bits = nf.bit_length() - 1
    hops = bits - 1
    all_heads = width // HD
    heads = all_heads // nz
    anchor_total = anchors.shape[0]
    total = nz * (1 + anchor_total)
    listed = block_ids.shape[2]
    tile = (BLOCK, HD)
    bf = jnp.bfloat16
    dma = pltpu.SemaphoreType.DMA
    smem = pl.BlockSpec(memory_space=pltpu.SMEM)
    vmem = pl.BlockSpec(memory_space=pltpu.VMEM)
    return pl.pallas_call(
        functools.partial(kernel, nz, nf, bits, heads, anchor_total, listed),
        out_shape=jax.ShapeDtypeStruct((rows, width), bf),
        in_specs=[smem] * 3 + [pl.BlockSpec(memory_space=pl.ANY)] * 3 + [vmem] * 2,
        out_specs=vmem,
        scratch_shapes=[
            pltpu.VMEM((rows, width), bf),
            pltpu.VMEM((rows, width), bf),
            pltpu.VMEM((rows, width), bf),
            dma((3,)),
            pltpu.VMEM((all_heads,) + tile, bf),
            pltpu.VMEM((all_heads,) + tile, bf),
            pltpu.VMEM((2, heads, total) + tile, bf),
            pltpu.VMEM((heads, nz) + tile, bf),
            pltpu.VMEM((heads, nz) + tile, bf),
            pltpu.VMEM((hops, heads, anchor_total, nz) + tile, bf),
            pltpu.VMEM((hops, heads, anchor_total, nz) + tile, bf),
            pltpu.VMEM((heads, nz) + tile, bf),
            pltpu.VMEM((nz, 8, total * BLOCK), jnp.float32),
            dma((3, heads, nz)),
            dma((3, heads, nz)),
            dma((heads,)),
            dma((heads,)),
            dma((hops, heads)),
            dma((hops, heads)),
            dma((heads,)),
            dma((heads,)),
            dma((heads, nz)),
            dma((heads, nz)),
        ],
        compiler_params=pltpu.CompilerParams(
            collective_id=0, has_side_effects=True, vmem_limit_bytes=56 * 1024 * 1024
        ),
    )(block_ids, counts, anchors, queries, keys, values, q_gain[None, :], k_gain[None, :])


def solution(mesh):
    placed = (
        P(("frame", "head"), None),
        P(("frame", "head"), None),
        P(("frame", "head"), None),
        P(),
        P(),
        P("frame", None, None),
        P("frame", None),
        P(),
    )
    return jax.shard_map(
        functools.partial(shards, mesh.shape["head"], mesh.shape["frame"]),
        mesh=mesh, in_specs=placed, out_specs=P(("frame", "head"), None), check_vma=False,
    )
```
